32 devices in a mesh: dp: 4 (over y, x), expert: 8 (over z, core).
Axes of the slice: x: 2, y: 2, z: 4, core: 2. Of those that a mesh axis runs over, the one named last changes fastest.
Arguments:
- tokens: bfloat16 [4096, 768], P(('dp', 'expert')), may hold values from -6 to 6
- cotangent: bfloat16 [4096, 768], P(('dp', 'expert')), may hold values from -6 to 6
- routes: int32 [4096, 2], P(('dp', 'expert')), may hold values from 0 to 7, all different within a row; in each aligned block of 128 rows (0 to 127, 128 to 255, ...) at most 96 rows name the same one
- gates: float32 [4096, 2], P(('dp', 'expert')), may hold values from 0.1 to 1
- w_in: bfloat16 [8, 2304, 768], P('expert', 'dp'), may hold values from -0.21875 to 0.21875
- w_out: bfloat16 [8, 2304, 768], P('expert', 'dp'), may hold values from -0.125 to 0.125
Outputs:
- d_tokens: bfloat16 [4096, 768], P(('dp', 'expert'))
- grad_in: float32 [8, 2304, 768], P('expert', 'dp')
- grad_out: float32 [8, 2304, 768], P('expert', 'dp')
The draws below stay inside these ranges and needn't reach their ends.
Inputs may be any that keep to these rules, and one draw needn't show every extreme that they name: `routes`: within the rows of one device (128 rows) no expert is named more than 96 times, and in every draw some expert is named exactly 96 times by the rows of some device; the 2 entries of a row differ.
All inputs are finite; a program needn't handle non-finite values.
Results may differ from the reference program's by a relative error of at most 0.015.
Values may be sent and summed in bfloat16 or wider, within the bound.
A program may use at most 64 MiB of HBM per device.

```python
import math
import jax
import jax.numpy as jnp
import numpy as np
from jax import lax

D = 768
HID = 2304
TOPK = 2
TOK_DEV = 128
EXPERTS = 8
CAP = 96
TOKENS = 4096
N_DP = 4


def block_levels(stream_key, dims, split, least, high):
    def one(axis_at, shards_of):
        heights = jax.random.uniform(jax.random.fold_in(jax.random.fold_in(stream_key, 6), axis_at), (shards_of,), jnp.float32, least / len(split), high / len(split))
        return jnp.repeat(jnp.exp(heights), dims[axis_at] // shards_of).reshape((-1,) + (1,) * (len(dims) - axis_at - 1))

    factor_of = one(*split[0])
    for cut in split[1:]:
        factor_of = factor_of * one(*cut)
    return factor_of


def assign_block(rng, own, number, rows, amount, top, most, skew):
    sequence = jax.random.permutation(rng, amount)
    crowded, common = shares(amount, rows * top, most, skew, True), shares(amount, rows * top, most, skew, False)
    places = jnp.arange(amount)

    def named(tallies, rotation):
        used = int((tallies > 0).sum())
        fixed = max(1, used // 4)
        shifted = fixed + (places - fixed + rotation * (used - fixed)) % max(1, amount - fixed)
        return jnp.zeros((amount,), jnp.int32).at[sequence[jnp.where(places < fixed, places, shifted)]].set(jnp.asarray(tallies, jnp.int32))

    tallies = jnp.where(number % 4 == 0, named(crowded, number // 4), named(common, number - number // 4 - 1))
    mixed = jax.random.permutation(jax.random.fold_in(own, 3), amount)
    giver, taker = mixed[0:amount // 2 * 2:2], mixed[1:amount // 2 * 2:2]
    slack = jnp.minimum(tallies[giver] - 1, most - tallies[taker]) // 2
    slack = jnp.where((giver == sequence[0]) | (taker == sequence[0]) | (tallies[taker] == 0), 0, jnp.maximum(slack, 0))
    shifted = jax.random.randint(jax.random.fold_in(own, 4), (amount // 2,), 0, 1 << 20) % (slack + 1)
    tallies = tallies.at[giver].add(-shifted).at[taker].add(shifted)
    labels = jnp.searchsorted(jnp.cumsum(tallies), jnp.arange(rows * top), side="right").astype(jnp.int32)
    table = labels.reshape(top, rows).T
    table = table[jax.random.permutation(jax.random.fold_in(own, 1), rows)]
    rotation = jax.random.randint(jax.random.fold_in(own, 2), (rows, 1), 0, top)
    return jnp.take_along_axis(table, (jnp.arange(top)[None, :] + rotation) % top, axis=1)


def shares(count, total, bound, slope, full):
    weights = [(1 << 20) // math.isqrt(standing ** slope) + 1 for standing in range(1, count + 1)]
    largest = bound if full else min(bound, max(-(-total // count), total * weights[0] // sum(weights)))
    least = 1 if total - largest >= count - 1 else 0
    counts, rest = [largest] + [least] * (count - 1), total - largest - least * (count - 1)
    while rest > 0:
        free = [i for i in range(1, count) if counts[i] < largest] or [i for i in range(1, count) if counts[i] < bound]
        mass, budget = sum([weights[i] for i in free]), rest
        for i in free:
            extra = min(bound - counts[i], max(1, budget * weights[i] // mass), rest)
            counts[i] = counts[i] + extra
            rest = rest - extra
    return np.array(counts)


def gaussian(rng, extent, scale, limit, pieces=(), kind=jnp.bfloat16):
    array = jax.random.normal(rng, extent, jnp.float32) * scale
    if len(pieces) > 0:
        array = block_levels(rng, extent, pieces, -0.22, 0.18) * array
    return jnp.clip(array, min=-limit, max=limit).astype(kind)


def setup_inputs(seed: int = 0) -> dict:
    arg_keys = jax.random.split(jax.random.key(seed), 7)
    tokens = gaussian(arg_keys[0], (TOKENS, D), 1.0, 6.0, ((0, 32),))
    cotangent = gaussian(arg_keys[1], (TOKENS, D), 1.0, 6.0, ((0, 32),))
    routes_keys = jax.random.split(jax.random.fold_in(arg_keys[2], 1), TOKENS // TOK_DEV)
    routes_turns = jax.random.permutation(jax.random.fold_in(arg_keys[2], 3), TOKENS // TOK_DEV)
    routes = jax.vmap(lambda own, number: assign_block(jax.random.fold_in(arg_keys[2], 2), own, number, TOK_DEV, EXPERTS, TOPK, CAP, 2))(routes_keys, routes_turns).reshape((TOKENS, TOPK))
    gates = jnp.clip(jnp.exp(math.log(1.0) - 2.3025851 * jax.random.uniform(arg_keys[3], (TOKENS, TOPK), jnp.float32) ** block_levels(arg_keys[3], (TOKENS, TOPK), ((0, 32),), -0.2, 0.2)), 0.1, 1.0)
    w_in = gaussian(arg_keys[4], (EXPERTS, HID, D), D ** -0.5, 0.21875, ((0, 8), (1, 4)))
    w_out = gaussian(arg_keys[5], (EXPERTS, HID, D), HID ** -0.5, 0.125, ((0, 8), (1, 4)))
    return {"tokens": tokens, "cotangent": cotangent, "routes": routes, "gates": gates, "w_in": w_in, "w_out": w_out}


tanh_coef = 0.7978845608028654
cubic_coef = 0.044715


def gelu_tanh(value):
    inner = tanh_coef * (value + cubic_coef * value * value * value)
    return 0.5 * value * (1.0 + jnp.tanh(inner))


def gelu_slope(value):
    inner = tanh_coef * (value + cubic_coef * value * value * value)
    slope_t = jnp.tanh(inner)
    return 0.5 * (1.0 + slope_t) + 0.5 * value * (1.0 - slope_t * slope_t) * tanh_coef * (1.0 + 3.0 * cubic_coef * value * value)


def dispatch_tables(route_blk, gate_blk, experts, capacity):
    tok_rows = route_blk.shape[0]
    flat = route_blk.reshape(-1)
    onehot = (flat[:, None] == jnp.arange(experts, dtype=jnp.int32)[None, :]).astype(jnp.int32)
    before = jnp.cumsum(onehot, axis=0) - onehot
    position = jnp.sum(before * onehot, axis=1).astype(jnp.int32)
    slots = (flat * capacity + position).reshape(tok_rows, -1)
    slot_ids = jnp.arange(experts * capacity, dtype=jnp.int32)
    placed = slot_ids[:, None, None] == slots[None, :, :]
    route_mat = jnp.sum(placed.astype(jnp.float32), axis=2)
    gate_slot = jnp.sum(jnp.where(placed, gate_blk[None, :, :], jnp.float32(0.0)), axis=(1, 2))
    return route_mat, gate_slot


def expert_backward(operands):
    rows_in, grads_in, weight_in, weight_out = operands
    weight_in32 = weight_in.astype(jnp.float32)
    weight_out32 = weight_out.astype(jnp.float32)
    rows32 = rows_in.astype(jnp.float32)
    grads32 = grads_in.astype(jnp.float32)
    pre = jnp.dot(rows32, weight_in32.T)
    acts = gelu_tanh(pre).astype(jnp.bfloat16)
    grad_act = jnp.dot(grads32, weight_out32.T)
    dpre = (grad_act * gelu_slope(pre)).astype(jnp.bfloat16)
    dpre32 = dpre.astype(jnp.float32)
    slot_grads = jnp.dot(dpre32, weight_in32).astype(jnp.bfloat16)
    part_in = jnp.dot(dpre32.T, rows32).astype(jnp.bfloat16)
    part_out = jnp.dot(acts.astype(jnp.float32).T, grads32).astype(jnp.bfloat16)
    return slot_grads, part_in, part_out


def reference(tokens, cotangent, routes, gates, w_in, w_out):
    sources = EXPERTS
    tok_all = tokens.reshape(N_DP, sources, TOK_DEV, D)
    cot_all = cotangent.reshape(N_DP, sources, TOK_DEV, D)
    route_all = routes.reshape(N_DP, sources, TOK_DEV, TOPK)
    gate_all = gates.reshape(N_DP, sources, TOK_DEV, TOPK)

    def row_group(state_now, inputs):
        tok_blk, cot_blk, route_blk, gate_blk = inputs
        route_mat, gate_slot = jax.vmap(lambda rr, gg: dispatch_tables(rr, gg, EXPERTS, CAP))(route_blk, gate_blk)
        rows_sent = jnp.einsum("sct,std->scd", route_mat, tok_blk.astype(jnp.float32)).astype(jnp.bfloat16)
        grad_rows = jnp.einsum("sct,std->scd", route_mat, cot_blk.astype(jnp.float32))
        grads_sent = (gate_slot[:, :, None] * grad_rows).astype(jnp.bfloat16)
        rows_expert = rows_sent.reshape(sources, EXPERTS, CAP, D).transpose(1, 0, 2, 3).reshape(EXPERTS, sources * CAP, D)
        grads_expert = grads_sent.reshape(sources, EXPERTS, CAP, D).transpose(1, 0, 2, 3).reshape(EXPERTS, sources * CAP, D)
        slot_grads, part_in, part_out = lax.map(expert_backward, (rows_expert, grads_expert, w_in, w_out))
        returned = slot_grads.reshape(EXPERTS, sources, CAP, D).transpose(1, 0, 2, 3).reshape(sources, EXPERTS * CAP, D)
        token_grads = jnp.einsum("sct,scd->std", route_mat, returned.astype(jnp.float32)).astype(jnp.bfloat16)
        new_state = (state_now[0] + part_in.astype(jnp.float32), state_now[1] + part_out.astype(jnp.float32))
        return new_state, token_grads

    zero_grads = jnp.zeros((EXPERTS, HID, D), jnp.float32)
    (grad_in, grad_out), token_grads = lax.scan(row_group, (zero_grads, zero_grads), (tok_all, cot_all, route_all, gate_all))
    d_tokens = token_grads.reshape(TOKENS, D)
    return d_tokens, grad_in, grad_out
```

```python
import jax
import jax.numpy as jnp
from jax import lax
from jax.sharding import PartitionSpec as P

tanh_coef = 0.7978845608028654
cubic_coef = 0.044715


def gelu_tanh(value):
    inner = tanh_coef * (value + cubic_coef * value * value * value)
    return 0.5 * value * (1.0 + jnp.tanh(inner))


def gelu_slope(value):
    inner = tanh_coef * (value + cubic_coef * value * value * value)
    slope_t = jnp.tanh(inner)
    return 0.5 * (1.0 + slope_t) + 0.5 * value * (1.0 - slope_t * slope_t) * tanh_coef * (
        1.0 + 3.0 * cubic_coef * value * value
    )


def dispatch_tables(route_blk, gate_blk, experts, capacity):
    tok_rows = route_blk.shape[0]
    flat = route_blk.reshape(-1)
    onehot = (flat[:, None] == jnp.arange(experts, dtype=jnp.int32)[None, :]).astype(jnp.int32)
    before = jnp.cumsum(onehot, axis=0) - onehot
    position = jnp.sum(before * onehot, axis=1)
    slots = (flat * capacity + position).reshape(tok_rows, -1)
    slot_ids = jnp.arange(experts * capacity, dtype=jnp.int32)
    placed = slot_ids[:, None, None] == slots[None, :, :]
    route_mat = jnp.sum(placed.astype(jnp.int32), axis=2).astype(jnp.bfloat16)
    gate_slot = jnp.sum(jnp.where(placed, gate_blk[None, :, :], jnp.float32(0.0)), axis=(1, 2))
    return (route_mat, gate_slot)


def exchange_sum(term, shard_rows):
    size = lax.axis_size("dp")
    me = lax.axis_index("dp")

    def piece(owner):
        return lax.dynamic_slice_in_dim(term, owner * shard_rows, shard_rows, 0)

    received = [
        lax.ppermute(piece(me ^ step), "dp", [(src, src ^ step) for src in range(size)])
        for step in range(1, size)
    ]
    total = piece(me).astype(jnp.float32)
    for block in received:
        total = total + block.astype(jnp.float32)
    return total


def shards(tokens, cotangent, routes, gates, w_in, w_out):
    experts = lax.axis_size("expert")
    tok_rows, model_width = tokens.shape
    top_count = routes.shape[1]
    capacity = 3 * tok_rows * top_count // experts
    shard_rows = w_in.shape[1]
    slot_rows = experts * capacity
    route_mat, gate_slot = dispatch_tables(routes, gates, experts, capacity)
    rows_sent = jnp.dot(route_mat, tokens, preferred_element_type=jnp.float32).astype(jnp.bfloat16)
    grad_rows = jnp.dot(route_mat, cotangent, preferred_element_type=jnp.float32)
    grads_sent = (gate_slot[:, None] * grad_rows).astype(jnp.bfloat16)
    rows_recv, grads_recv = (
        lax.all_to_all(
            rows_sent.reshape(experts, capacity, model_width),
            "expert",
            split_axis=0,
            concat_axis=0,
            tiled=True,
        ),
        lax.all_to_all(
            grads_sent.reshape(experts, capacity, model_width),
            "expert",
            split_axis=0,
            concat_axis=0,
            tiled=True,
        ),
    )
    rows_in = rows_recv.reshape(slot_rows, model_width)
    grads_in = grads_recv.reshape(slot_rows, model_width)
    piece_in = lax.all_gather(w_in[0], "dp", axis=0, tiled=True)
    piece_out = lax.all_gather(w_out[0], "dp", axis=0, tiled=True)
    pre = lax.dot_general(
        rows_in, piece_in, (((1,), (1,)), ((), ())), preferred_element_type=jnp.float32
    )
    acts = gelu_tanh(pre).astype(jnp.bfloat16)
    grad_act = lax.dot_general(
        grads_in, piece_out, (((1,), (1,)), ((), ())), preferred_element_type=jnp.float32
    )
    dpre = (grad_act * gelu_slope(pre)).astype(jnp.bfloat16)
    slot_sum = jnp.dot(dpre, piece_in, preferred_element_type=jnp.float32)
    slot_sum, acts_all, dpre_all = (slot_sum, acts, dpre)
    returned = lax.all_to_all(
        slot_sum.astype(jnp.bfloat16).reshape(experts, capacity, model_width),
        "expert",
        split_axis=0,
        concat_axis=0,
        tiled=True,
    )
    token_grads = lax.dot_general(
        route_mat,
        returned.reshape(slot_rows, model_width),
        (((0,), (0,)), ((), ())),
        preferred_element_type=jnp.float32,
    )
    d_tokens = token_grads.astype(jnp.bfloat16)
    term_in = lax.dot_general(
        dpre_all, rows_in, (((0,), (0,)), ((), ())), preferred_element_type=jnp.float32
    )
    term_out = lax.dot_general(
        acts_all, grads_in, (((0,), (0,)), ((), ())), preferred_element_type=jnp.float32
    )
    grad_out = exchange_sum(term_out.astype(jnp.bfloat16), shard_rows)[None]
    grad_in = exchange_sum(term_in.astype(jnp.bfloat16), shard_rows)[None]
    return (d_tokens, grad_in, grad_out)


def solution(mesh):
    in_specs = (
        P(("dp", "expert"), None),
        P(("dp", "expert"), None),
        P(("dp", "expert"), None),
        P(("dp", "expert"), None),
        P("expert", "dp", None),
        P("expert", "dp", None),
    )
    out_specs = (P(("dp", "expert"), None), P("expert", "dp", None), P("expert", "dp", None))
    return jax.shard_map(shards, mesh=mesh, in_specs=in_specs, out_specs=out_specs, check_vma=False)
```
